256 devices in a mesh: rows: 32 (over z_lo, y, x), cols: 8 (over z_hi, core).
Axes of the slice: x: 4, y: 4, z: 8 (z_hi: 4, z_lo: 2; z = z_hi * 2 + z_lo), core: 2. Of those that a mesh axis runs over, the one named last changes fastest.
Arguments:
- offsets: int32 [32, 131072], P('cols', 'rows'), may hold values from -1024 to 1024
- weights: float32 [32, 131072], P('cols', 'rows'), may hold values from 0.004 to 0.06
- seeds: float32 [64, 131072], P(None, ('rows', 'cols')), may hold values from -6 to 6
Outputs:
- scores: float32 [64, 131072], P(None, ('rows', 'cols'))
The draws below stay inside these ranges and needn't reach their ends.
All inputs are finite; a program needn't handle non-finite values.
Results may differ from the reference program's by a relative error of at most 0.00007.
Values sent between devices are 32-bit elements; how exact they have to be, the bound alone decides.
No kernel may reach another device: no remote copies, remote signals or barrier semaphores. Data moves between devices by JAX's collectives and lax.ppermute only.
A program may use at most 64 MiB of HBM per device.

```python
import math
import jax
import jax.numpy as jnp
from jax import lax

C = 64
K = 32
ITERS = 3
HW = 1024
N = 131072


def with_ends(result, own_key, least, high):
    longest = result.shape.index(max(result.shape))
    spots = []
    for shift in (0, 1):
        where = [jax.random.randint(jax.random.fold_in(own_key, axis), (), 0, length) for axis, length in enumerate(result.shape)]
        where[longest] = (where[longest] + shift) % result.shape[longest]
        spots.append(tuple(where))
    return result.at[spots[0]].set(least).at[spots[1]].set(high)


def block_scale(stream_key, extent, shards, least, high):
    level, own = 1.0, jax.random.fold_in(stream_key, 6)
    for position, parts in shards:
        draws = jnp.exp(jax.random.uniform(jax.random.fold_in(own, position), (parts,), jnp.float32, least / len(shards), high / len(shards)))
        level = level * jnp.repeat(draws, extent[position] // parts).reshape([-1 if axis == position else 1 for axis in range(len(extent))])
    return level


def bell_draw(stream_key, dims, deviation, most, split=(), kind=jnp.bfloat16):
    loudness = block_scale(stream_key, dims, split, -0.22, 0.18) if split else 1.0
    array = jax.random.normal(stream_key, dims, jnp.float32) * deviation * loudness
    return jnp.minimum(jnp.maximum(array, -most), most).astype(kind)


def setup_inputs(seed: int = 0) -> dict:
    key_of = jax.random.split(jax.random.key(seed), 4)
    return {
        "offsets": with_ends(jax.random.randint(key_of[0], (K, N), 0 - HW, HW + 1), jax.random.fold_in(key_of[0], 1), 0 - HW, HW).astype(jnp.int32),
        "weights": jnp.clip(jnp.exp(math.log(0.06) - 2.70805 * jax.random.uniform(key_of[1], (K, N), jnp.float32) ** block_scale(key_of[1], (K, N), ((0, 8), (1, 32)), -0.2, 0.2)), 0.004, 0.06),
        "seeds": bell_draw(key_of[2], (C, N), 1.0, 6.0, ((1, 256),), jnp.float32),
    }


def diffuse(panel, offsets, weights):
    padded = jnp.pad(panel, ((0, 0), (HW, HW)))
    places = jnp.arange(N, dtype=jnp.int32) + HW

    def add_slot(total, slot):
        index = places + offsets[slot]
        return total + weights[slot][None, :] * jnp.take(padded, index, axis=1)

    total = jnp.zeros(panel.shape, jnp.float32)
    total = lax.fori_loop(0, K, lambda slot, acc: add_slot(acc, slot), total)
    return total


def reference(offsets, weights, seeds):
    panel = seeds
    for step in range(ITERS):
        panel = 0.9 * diffuse(panel, offsets, weights) + 0.1 * seeds
    return panel
```

```python
import functools

import jax
import jax.numpy as jnp
from jax import lax
from jax.experimental import pallas as pl
from jax.experimental.pallas import tpu as pltpu
from jax.sharding import PartitionSpec as P

HW = 1024
ITERS = 3
LANES = 128
BLOCK = 256
TILES = (BLOCK + 2 * HW) // LANES
SPAN = TILES * LANES
AXES = ("rows", "cols")
NT = (((1,), (1,)), ((), ()))


def build_kernel(edges_ref, high_ref, low_ref, tile_ref, lane_ref, whigh_ref, wlow_ref):
    events = edges_ref.shape[1]
    lane = lax.broadcasted_iota(jnp.int32, (LANES, LANES), 1)
    row = lax.broadcasted_iota(jnp.int32, (LANES, LANES), 0)
    is_offset = (lane & 4) == 0
    for part in range(events // LANES):
        rows = slice(part * LANES, (part + 1) * LANES)
        cells = edges_ref[:, rows]
        turned = jnp.concatenate([cells, cells], axis=0).T
        offset = jnp.where(is_offset, turned, pltpu.roll(turned, 4, 1)).astype(jnp.int32)
        weight = jnp.where(is_offset, pltpu.roll(turned, LANES - 4, 1), turned)
        place = offset + row + (HW + part * LANES % BLOCK)
        tile_ref[rows] = (place >> 7).astype(jnp.float32)
        lane_ref[rows] = (place & (LANES - 1)).astype(jnp.float32)
        high = weight.astype(jnp.bfloat16).astype(jnp.float32)
        whigh_ref[rows] = high
        wlow_ref[rows] = weight - high

    sub = lax.broadcasted_iota(jnp.int32, (8, LANES), 0)
    lane8 = lax.broadcasted_iota(jnp.int32, (8, LANES), 1)
    owner = (lane8 >> 6) * 2 + ((lane8 >> 2) & 1)
    masks = [sub == owner, sub == owner + 4]
    lane_ids = lax.broadcasted_iota(jnp.int32, (LANES, LANES), 0).astype(jnp.float32).astype(jnp.bfloat16)
    two = lax.broadcasted_iota(jnp.int32, (16, LANES), 0)
    two = (two >> 3).astype(jnp.float32).astype(jnp.bfloat16)
    one = jnp.ones((), jnp.bfloat16)
    zero = jnp.zeros((), jnp.bfloat16)

    def eight(at):
        tile, lanes, whigh, wlow = (ref[pl.ds(at, 8), :] for ref in (tile_ref, lane_ref, whigh_ref, wlow_ref))
        twice = lambda x: jnp.concatenate([x, x], axis=0).astype(jnp.bfloat16)
        wh, wl = twice(whigh), twice(wlow)
        left, right = [], []
        highs, lows = [], []
        for mask in masks:
            mine = twice(jnp.where(mask, tile, -1.0)) - two
            hits = [mine == jnp.asarray(2.0 * step, jnp.bfloat16) for step in range(TILES // 2)]
            highs.append(jnp.concatenate([jnp.where(hit, wh, zero) for hit in hits], axis=0))
            lows.append(jnp.concatenate([jnp.where(hit, wl, zero) for hit in hits], axis=0))
            spot = jnp.sum(jnp.where(mask, lanes, 0.0), axis=0, keepdims=True)
            spot = jnp.broadcast_to(spot, (LANES, LANES)).astype(jnp.bfloat16)
            right.append(jnp.where(spot == lane_ids, one, zero))
        left = jnp.concatenate(highs + lows, axis=1)
        right = jnp.concatenate(right + right, axis=1)
        return lax.dot_general(left, right, NT, preferred_element_type=jnp.float32)

    def sixteen(turn, _):
        at = pl.multiple_of(turn * 16, 16)
        first, second = eight(at), eight(at + 8)
        for step in range(TILES):
            both = jnp.concatenate([first[step * 8:step * 8 + 8], second[step * 8:step * 8 + 8]], axis=0)
            high = both.astype(jnp.bfloat16)
            columns = slice(step * LANES, (step + 1) * LANES)
            high_ref[pl.ds(at, 16), columns] = high
            low_ref[pl.ds(at, 16), columns] = (both - high.astype(jnp.float32)).astype(jnp.bfloat16)
        return 0

    lax.fori_loop(0, events // 16, sixteen, 0)


def build(edges):
    events = edges.shape[1]
    out = jax.ShapeDtypeStruct((events, SPAN), jnp.bfloat16)
    return pl.pallas_call(
        build_kernel,
        out_shape=(out, out),
        scratch_shapes=[pltpu.VMEM((events, LANES), jnp.float32)] * 4,
        compiler_params=pltpu.CompilerParams(vmem_limit_bytes=32 * 2**20),
        name="build",
    )(edges)


def apply_kernel(high_ref, low_ref, seeds_ref, *refs):
    *panel_refs, out_ref, window_ref = refs
    channels, events = out_ref.shape
    for number, ref in enumerate(panel_refs):
        value = ref[...]
        high = value.astype(jnp.bfloat16)
        columns = slice(number * events, (number + 1) * events)
        window_ref[:channels, columns] = high
        window_ref[channels:, columns] = (value - high.astype(jnp.float32)).astype(jnp.bfloat16)
    for part in range(events // BLOCK):
        rows = slice(part * BLOCK, (part + 1) * BLOCK)
        window = window_ref[:, part * BLOCK:part * BLOCK + SPAN]
        both = lax.dot_general(window, high_ref[rows], NT, preferred_element_type=jnp.float32)
        rest = lax.dot_general(window[:channels], low_ref[rows], NT, preferred_element_type=jnp.float32)
        total = both[:channels] + (both[channels:] + rest)
        out_ref[:, rows] = 0.9 * total + 0.1 * seeds_ref[:, rows]


def apply(matrix, seeds, panels):
    channels, events = seeds.shape
    return pl.pallas_call(
        apply_kernel,
        out_shape=jax.ShapeDtypeStruct(seeds.shape, jnp.float32),
        scratch_shapes=[pltpu.VMEM((2 * channels, len(panels) * events), jnp.bfloat16)],
        compiler_params=pltpu.CompilerParams(vmem_limit_bytes=32 * 2**20),
        name="apply",
    )(*matrix, seeds, *panels)


def shifted(cells, step, count):
    pairs = [(i, i + step) for i in range(count) if 0 <= i + step < count]
    return lax.ppermute(cells, AXES, pairs)


def on_device(offsets, weights, seeds, *, count):
    reach = HW // seeds.shape[1]
    edges = jnp.concatenate([offsets.astype(jnp.float32), weights], axis=0)
    edges = lax.all_to_all(edges, "cols", split_axis=1, concat_axis=0, tiled=True)
    matrix = build(edges)
    scores = seeds
    for _ in range(ITERS):
        before = [shifted(scores, step, count) for step in range(reach, 0, -1)]
        after = [shifted(scores, -step, count) for step in range(1, reach + 1)]
        scores = apply(matrix, seeds, [*before, scores, *after])
    return scores


def solution(mesh):
    count = mesh.shape["rows"] * mesh.shape["cols"]
    in_specs = (P("cols", "rows"), P("cols", "rows"), P(None, AXES))
    return jax.shard_map(
        functools.partial(on_device, count=count),
        mesh=mesh, in_specs=in_specs, out_specs=P(None, AXES), check_vma=False,
    )
```

```python
import functools

import jax
import jax.numpy as jnp
from jax import lax
from jax.experimental import pallas as pl
from jax.experimental.pallas import tpu as pltpu
from jax.sharding import PartitionSpec as P

HW = 1024
ITERS = 3
LANES = 128
BLOCK = 256
TILES = (BLOCK + 2 * HW) // LANES
SPAN = TILES * LANES
AXES = ("rows", "cols")
NT = (((1,), (1,)), ((), ()))


def build_kernel(edges_ref, high_ref, low_ref, tile_ref, lane_ref, whigh_ref, wlow_ref):
    events = edges_ref.shape[1]
    lane = lax.broadcasted_iota(jnp.int32, (LANES, LANES), 1)
    row = lax.broadcasted_iota(jnp.int32, (LANES, LANES), 0)
    is_offset = (lane & 4) == 0
    for part in range(events // LANES):
        rows = slice(part * LANES, (part + 1) * LANES)
        cells = edges_ref[:, rows]
        turned = jnp.concatenate([cells, cells], axis=0).T
        offset = jnp.where(is_offset, turned, pltpu.roll(turned, 4, 1)).astype(jnp.int32)
        weight = jnp.where(is_offset, pltpu.roll(turned, LANES - 4, 1), turned)
        place = offset + row + (HW + part * LANES % BLOCK)
        tile_ref[rows] = (place >> 7).astype(jnp.float32)
        lane_ref[rows] = (place & (LANES - 1)).astype(jnp.float32)
        high = weight.astype(jnp.bfloat16).astype(jnp.float32)
        whigh_ref[rows] = high
        wlow_ref[rows] = weight - high

    sub = lax.broadcasted_iota(jnp.int32, (8, LANES), 0)
    lane8 = lax.broadcasted_iota(jnp.int32, (8, LANES), 1)
    owner = (lane8 >> 6) * 2 + ((lane8 >> 2) & 1)
    masks = [sub == owner, sub == owner + 4]
    lane_ids = lax.broadcasted_iota(jnp.int32, (LANES, LANES), 0).astype(jnp.float32).astype(jnp.bfloat16)
    two = lax.broadcasted_iota(jnp.int32, (16, LANES), 0)
    two = (two >> 3).astype(jnp.float32).astype(jnp.bfloat16)
    one = jnp.ones((), jnp.bfloat16)
    zero = jnp.zeros((), jnp.bfloat16)

    def eight(at):
        tile, lanes, whigh, wlow = (ref[pl.ds(at, 8), :] for ref in (tile_ref, lane_ref, whigh_ref, wlow_ref))
        twice = lambda x: jnp.concatenate([x, x], axis=0).astype(jnp.bfloat16)
        wh, wl = twice(whigh), twice(wlow)
        left, right = [], []
        highs, lows = [], []
        for mask in masks:
            mine = twice(jnp.where(mask, tile, -1.0)) - two
            hits = [mine == jnp.asarray(2.0 * step, jnp.bfloat16) for step in range(TILES // 2)]
            highs.append(jnp.concatenate([jnp.where(hit, wh, zero) for hit in hits], axis=0))
            lows.append(jnp.concatenate([jnp.where(hit, wl, zero) for hit in hits], axis=0))
            spot = jnp.sum(jnp.where(mask, lanes, 0.0), axis=0, keepdims=True)
            spot = jnp.broadcast_to(spot, (LANES, LANES)).astype(jnp.bfloat16)
            right.append(jnp.where(spot == lane_ids, one, zero))
        left = jnp.concatenate(highs + lows, axis=1)
        right = jnp.concatenate(right + right, axis=1)
        return lax.dot_general(left, right, NT, preferred_element_type=jnp.float32)

    def sixteen(turn, _):
        at = pl.multiple_of(turn * 16, 16)
        first, second = eight(at), eight(at + 8)
        for step in range(TILES):
            both = jnp.concatenate([first[step * 8:step * 8 + 8], second[step * 8:step * 8 + 8]], axis=0)
            high = both.astype(jnp.bfloat16)
            columns = slice(step * LANES, (step + 1) * LANES)
            high_ref[pl.ds(at, 16), columns] = high
            low_ref[pl.ds(at, 16), columns] = (both - high.astype(jnp.float32)).astype(jnp.bfloat16)
        return 0

    lax.fori_loop(0, events // 16, sixteen, 0)


def build(edges):
    events = edges.shape[1]
    out = jax.ShapeDtypeStruct((events, SPAN), jnp.bfloat16)
    return pl.pallas_call(
        build_kernel,
        out_shape=(out, out),
        scratch_shapes=[pltpu.VMEM((events, LANES), jnp.float32)] * 4,
        compiler_params=pltpu.CompilerParams(vmem_limit_bytes=32 * 2**20),
        cost_estimate=pl.CostEstimate(flops=8 * 32 * events * SPAN * 4, bytes_accessed=4 * events * SPAN, transcendentals=0),
        name="build",
    )(edges)


def apply_kernel(high_ref, low_ref, seeds_ref, own_ref, pair_ref, far_ref, cross_ref, out_ref, window_ref):
    channels, events = out_ref.shape
    second = lax.axis_index("cols") % 2
    blocks = [own_ref[...], pair_ref[...], cross_ref[...], far_ref[:channels], far_ref[channels:]]
    for value, place in zip(blocks, (2, 3, 4, 1, 0)):
        at = pl.multiple_of((place + second * (4 - 2 * place)) * events, events)
        high = value.astype(jnp.bfloat16)
        window_ref[:channels, pl.ds(at, events)] = high
        window_ref[channels:, pl.ds(at, events)] = (value - high.astype(jnp.float32)).astype(jnp.bfloat16)
    for part in range(events // BLOCK):
        rows = slice(part * BLOCK, (part + 1) * BLOCK)
        window = window_ref[:, part * BLOCK:part * BLOCK + SPAN]
        both = lax.dot_general(window, high_ref[rows], NT, preferred_element_type=jnp.float32)
        rest = lax.dot_general(window[:channels], low_ref[rows], NT, preferred_element_type=jnp.float32)
        total = both[:channels] + (both[channels:] + rest)
        out_ref[:, rows] = 0.9 * total + 0.1 * seeds_ref[:, rows]


def apply(matrix, seeds, panels):
    channels, events = seeds.shape
    return pl.pallas_call(
        apply_kernel,
        out_shape=jax.ShapeDtypeStruct(seeds.shape, jnp.float32),
        scratch_shapes=[pltpu.VMEM((2 * channels, 5 * events), jnp.bfloat16)],
        compiler_params=pltpu.CompilerParams(vmem_limit_bytes=32 * 2**20),
        cost_estimate=pl.CostEstimate(flops=6 * channels * events * SPAN, bytes_accessed=4 * events * SPAN, transcendentals=0),
        name="apply",
    )(*matrix, seeds, *panels)


def pack_kernel(offsets_ref, weights_ref, out_ref):
    slots = offsets_ref.shape[0]
    out_ref[:slots] = offsets_ref[...].astype(jnp.float32)
    out_ref[slots:] = weights_ref[...]


def pack(offsets, weights):
    slots, events = offsets.shape
    return pl.pallas_call(
        pack_kernel,
        out_shape=jax.ShapeDtypeStruct((2 * slots, events), jnp.float32),
        name="pack",
    )(offsets, weights)


def on_device(offsets, weights, seeds, *, count):
    channels = seeds.shape[0]
    on_chip = [(i, i ^ 1) for i in range(count)]
    off_chip = [(i, i + 1 if i % 2 else i - 1) for i in range(1, count - 1)]
    edges = pack(offsets, weights)
    edges = lax.all_to_all(edges, "cols", split_axis=1, concat_axis=0, tiled=True)
    matrix = build(edges)
    scores = seeds
    for _ in range(ITERS):
        pair = lax.ppermute(scores, AXES, on_chip)
        far = lax.ppermute(jnp.concatenate([scores, pair], axis=0), AXES, off_chip)
        cross = lax.ppermute(far[:channels], AXES, on_chip)
        scores = apply(matrix, seeds, [scores, pair, far, cross])
    return scores


def solution(mesh):
    count = mesh.shape["rows"] * mesh.shape["cols"]
    in_specs = (P("cols", "rows"), P("cols", "rows"), P(None, AXES))
    return jax.shard_map(
        functools.partial(on_device, count=count),
        mesh=mesh, in_specs=in_specs, out_specs=P(None, AXES), check_vma=False,
    )
```

```python
import functools

import jax
import jax.numpy as jnp
from jax import lax
from jax.experimental import pallas as pl
from jax.experimental.pallas import tpu as pltpu
from jax.sharding import PartitionSpec as P

HW = 1024
ITERS = 3
LANES = 128
BLOCK = 256
TILES = (BLOCK + 2 * HW) // LANES
SPAN = TILES * LANES
AXES = ("rows", "cols")
NT = (((1,), (1,)), ((), ()))


def build_kernel(edges_ref, high_ref, low_ref, tile_ref, lane_ref, whigh_ref, wlow_ref):
    events = edges_ref.shape[1]
    lane = lax.broadcasted_iota(jnp.int32, (LANES, LANES), 1)
    row = lax.broadcasted_iota(jnp.int32, (LANES, LANES), 0)
    is_offset = (lane & 4) == 0
    for part in range(events // LANES):
        rows = slice(part * LANES, (part + 1) * LANES)
        cells = edges_ref[:, rows]
        turned = jnp.concatenate([cells, cells], axis=0).T
        offset = jnp.where(is_offset, turned, pltpu.roll(turned, 4, 1)).astype(jnp.int32)
        weight = jnp.where(is_offset, pltpu.roll(turned, LANES - 4, 1), turned)
        place = offset + row + (HW + part * LANES % BLOCK)
        tile_ref[rows] = (place >> 7).astype(jnp.float32)
        lane_ref[rows] = (place & (LANES - 1)).astype(jnp.float32)
        high = weight.astype(jnp.bfloat16).astype(jnp.float32)
        whigh_ref[rows] = high
        wlow_ref[rows] = weight - high

    sub = lax.broadcasted_iota(jnp.int32, (8, LANES), 0)
    lane8 = lax.broadcasted_iota(jnp.int32, (8, LANES), 1)
    owner = (lane8 >> 6) * 2 + ((lane8 >> 2) & 1)
    masks = [sub == owner, sub == owner + 4]
    lane_ids = lax.broadcasted_iota(jnp.int32, (LANES, LANES), 0).astype(jnp.float32).astype(jnp.bfloat16)
    two = lax.broadcasted_iota(jnp.int32, (16, LANES), 0)
    two = (two >> 3).astype(jnp.float32).astype(jnp.bfloat16)
    one = jnp.ones((), jnp.bfloat16)
    zero = jnp.zeros((), jnp.bfloat16)

    def eight(at):
        tile, lanes, whigh, wlow = (ref[pl.ds(at, 8), :] for ref in (tile_ref, lane_ref, whigh_ref, wlow_ref))
        twice = lambda x: jnp.concatenate([x, x], axis=0).astype(jnp.bfloat16)
        wh, wl = twice(whigh), twice(wlow)
        left, right = [], []
        highs, lows = [], []
        for mask in masks:
            mine = twice(jnp.where(mask, tile, -1.0)) - two
            hits = [mine == jnp.asarray(2.0 * step, jnp.bfloat16) for step in range(TILES // 2)]
            highs.append(jnp.concatenate([jnp.where(hit, wh, zero) for hit in hits], axis=0))
            lows.append(jnp.concatenate([jnp.where(hit, wl, zero) for hit in hits], axis=0))
            spot = jnp.sum(jnp.where(mask, lanes, 0.0), axis=0, keepdims=True)
            spot = jnp.broadcast_to(spot, (LANES, LANES)).astype(jnp.bfloat16)
            right.append(jnp.where(spot == lane_ids, one, zero))
        left = jnp.concatenate(highs + lows, axis=1)
        right = jnp.concatenate(right + right, axis=1)
        return lax.dot_general(left, right, NT, preferred_element_type=jnp.float32)

    def sixteen(turn, _):
        at = pl.multiple_of(turn * 16, 16)
        first, second = eight(at), eight(at + 8)
        for step in range(TILES):
            both = jnp.concatenate([first[step * 8:step * 8 + 8], second[step * 8:step * 8 + 8]], axis=0)
            high = both.astype(jnp.bfloat16)
            columns = slice(step * LANES, (step + 1) * LANES)
            high_ref[pl.ds(at, 16), columns] = high
            low_ref[pl.ds(at, 16), columns] = (both - high.astype(jnp.float32)).astype(jnp.bfloat16)
        return 0

    lax.fori_loop(0, events // 16, sixteen, 0, unroll=8)


def build(edges):
    events = edges.shape[1]
    out = jax.ShapeDtypeStruct((events, SPAN), jnp.bfloat16)
    return pl.pallas_call(
        build_kernel,
        out_shape=(out, out),
        scratch_shapes=[pltpu.VMEM((events, LANES), jnp.float32)] * 4,
        compiler_params=pltpu.CompilerParams(vmem_limit_bytes=32 * 2**20),
        cost_estimate=pl.CostEstimate(flops=3000000000, bytes_accessed=4 * events * SPAN, transcendentals=0),
        name="build",
    )(edges)


def apply_kernel(high_ref, low_ref, seeds_ref, own_ref, pair_ref, far_ref, cross_ref, out_ref, window_ref):
    channels, events = out_ref.shape
    second = lax.axis_index("cols") % 2
    blocks = [own_ref[...], pair_ref[...], cross_ref[...], far_ref[:channels], far_ref[channels:]]
    for value, place in zip(blocks, (2, 3, 4, 1, 0)):
        at = pl.multiple_of((place + second * (4 - 2 * place)) * events, events)
        high = value.astype(jnp.bfloat16)
        window_ref[:channels, pl.ds(at, events)] = high
        window_ref[channels:, pl.ds(at, events)] = (value - high.astype(jnp.float32)).astype(jnp.bfloat16)
    for part in range(events // BLOCK):
        rows = slice(part * BLOCK, (part + 1) * BLOCK)
        window = window_ref[:, part * BLOCK:part * BLOCK + SPAN]
        both = lax.dot_general(window, high_ref[rows], NT, preferred_element_type=jnp.float32)
        rest = lax.dot_general(window[:channels], low_ref[rows], NT, preferred_element_type=jnp.float32)
        total = both[:channels] + (both[channels:] + rest)
        out_ref[:, rows] = 0.9 * total + 0.1 * seeds_ref[:, rows]


def apply(matrix, seeds, panels):
    channels, events = seeds.shape
    return pl.pallas_call(
        apply_kernel,
        out_shape=jax.ShapeDtypeStruct(seeds.shape, jnp.float32),
        scratch_shapes=[pltpu.VMEM((2 * channels, 5 * events), jnp.bfloat16)],
        compiler_params=pltpu.CompilerParams(vmem_limit_bytes=32 * 2**20),
        cost_estimate=pl.CostEstimate(flops=6 * channels * events * SPAN, bytes_accessed=4 * events * SPAN, transcendentals=0),
        name="apply",
    )(*matrix, seeds, *panels)


def pack_kernel(offsets_ref, weights_ref, out_ref):
    slots = offsets_ref.shape[0]
    out_ref[:slots] = offsets_ref[...].astype(jnp.float32)
    out_ref[slots:] = weights_ref[...]


def pack(offsets, weights):
    slots, events = offsets.shape
    return pl.pallas_call(
        pack_kernel,
        out_shape=jax.ShapeDtypeStruct((2 * slots, events), jnp.float32),
        name="pack",
    )(offsets, weights)


def on_device(offsets, weights, seeds, *, count):
    channels = seeds.shape[0]
    on_chip = [(i, i ^ 1) for i in range(count)]
    off_chip = [(i, i + 1 if i % 2 else i - 1) for i in range(1, count - 1)]
    edges = pack(offsets, weights)
    edges = lax.all_to_all(edges, "cols", split_axis=1, concat_axis=0, tiled=True)
    matrix = build(edges)
    scores = seeds
    for step in range(ITERS):
        pair = lax.ppermute(scores, AXES, on_chip)
        far = lax.ppermute(jnp.concatenate([scores, pair], axis=0), AXES, off_chip)
        if step == 0:
            far, *matrix = lax.optimization_barrier((far, *matrix))
        cross = lax.ppermute(far[:channels], AXES, on_chip)
        scores = apply(matrix, seeds, [scores, pair, far, cross])
    return scores


def solution(mesh):
    count = mesh.shape["rows"] * mesh.shape["cols"]
    in_specs = (P("cols", "rows"), P("cols", "rows"), P(None, AXES))
    return jax.shard_map(
        functools.partial(on_device, count=count),
        mesh=mesh, in_specs=in_specs, out_specs=P(None, AXES), check_vma=False,
    )
```

```python
import functools

import jax
import jax.numpy as jnp
from jax import lax
from jax.experimental import pallas as pl
from jax.experimental.pallas import tpu as pltpu
from jax.sharding import PartitionSpec as P

HW = 1024
ITERS = 3
LANES = 128
BLOCK = 256
TILES = (BLOCK + 2 * HW) // LANES
SPAN = TILES * LANES
AXES = ("rows", "cols")
NT = (((1,), (1,)), ((), ()))


def build_kernel(edges_ref, high_ref, low_ref, tile_ref, lane_ref, whigh_ref, wlow_ref):
    events = edges_ref.shape[1]
    lane = lax.broadcasted_iota(jnp.int32, (LANES, LANES), 1)
    row = lax.broadcasted_iota(jnp.int32, (LANES, LANES), 0)
    is_offset = (lane & 4) == 0
    for part in range(events // LANES):
        rows = slice(part * LANES, (part + 1) * LANES)
        cells = edges_ref[:, rows]
        turned = jnp.concatenate([cells, cells], axis=0).T
        offset = jnp.where(is_offset, turned, pltpu.roll(turned, 4, 1)).astype(jnp.int32)
        weight = jnp.where(is_offset, pltpu.roll(turned, LANES - 4, 1), turned)
        place = offset + row + (HW + part * LANES % BLOCK)
        tile_ref[rows] = (place >> 7).astype(jnp.float32)
        lane_ref[rows] = (place & (LANES - 1)).astype(jnp.float32)
        high = weight.astype(jnp.bfloat16).astype(jnp.float32)
        whigh_ref[rows] = high
        wlow_ref[rows] = weight - high

    sub = lax.broadcasted_iota(jnp.int32, (8, LANES), 0)
    lane8 = lax.broadcasted_iota(jnp.int32, (8, LANES), 1)
    owner = (lane8 >> 6) * 2 + ((lane8 >> 2) & 1)
    masks = [sub == owner, sub == owner + 4]
    lane_ids = lax.broadcasted_iota(jnp.int32, (LANES, LANES), 0).astype(jnp.float32).astype(jnp.bfloat16)
    two = lax.broadcasted_iota(jnp.int32, (16, LANES), 0)
    two = (two >> 3).astype(jnp.float32).astype(jnp.bfloat16)
    one = jnp.ones((), jnp.bfloat16)
    zero = jnp.zeros((), jnp.bfloat16)

    def eight(at):
        tile, lanes, whigh, wlow = (ref[pl.ds(at, 8), :] for ref in (tile_ref, lane_ref, whigh_ref, wlow_ref))
        twice = lambda x: jnp.concatenate([x, x], axis=0).astype(jnp.bfloat16)
        wh, wl = twice(whigh), twice(wlow)
        left, right = [], []
        highs, lows = [], []
        for mask in masks:
            mine = twice(jnp.where(mask, tile, -1.0)) - two
            hits = [mine == jnp.asarray(2.0 * step, jnp.bfloat16) for step in range(TILES // 2)]
            highs.append(jnp.concatenate([jnp.where(hit, wh, zero) for hit in hits], axis=0))
            lows.append(jnp.concatenate([jnp.where(hit, wl, zero) for hit in hits], axis=0))
            spot = jnp.sum(jnp.where(mask, lanes, 0.0), axis=0, keepdims=True)
            spot = jnp.broadcast_to(spot, (LANES, LANES)).astype(jnp.bfloat16)
            right.append(jnp.where(spot == lane_ids, one, zero))
        left = jnp.concatenate(highs + lows, axis=1)
        right = jnp.concatenate(right + right, axis=1)
        return lax.dot_general(left, right, NT, preferred_element_type=jnp.float32)

    def sixteen(turn, _):
        at = pl.multiple_of(turn * 16, 16)
        first, second = eight(at), eight(at + 8)
        for step in range(TILES):
            both = jnp.concatenate([first[step * 8:step * 8 + 8], second[step * 8:step * 8 + 8]], axis=0)
            high = both.astype(jnp.bfloat16)
            columns = slice(step * LANES, (step + 1) * LANES)
            high_ref[pl.ds(at, 16), columns] = high
            low_ref[pl.ds(at, 16), columns] = (both - high.astype(jnp.float32)).astype(jnp.bfloat16)
        return 0

    lax.fori_loop(0, events // 16, sixteen, 0, unroll=8)


def build(edges):
    events = edges.shape[1]
    out = jax.ShapeDtypeStruct((events, SPAN), jnp.bfloat16)
    return pl.pallas_call(
        build_kernel,
        out_shape=(out, out),
        scratch_shapes=[pltpu.VMEM((events, LANES), jnp.float32)] * 4,
        compiler_params=pltpu.CompilerParams(vmem_limit_bytes=32 * 2**20),
        cost_estimate=pl.CostEstimate(flops=3000000000, bytes_accessed=4 * events * SPAN, transcendentals=0),
        name="build",
    )(edges)


def apply_kernel(high_ref, low_ref, seeds_ref, *refs, places, count):
    *panel_refs, out_ref, window_ref = refs
    channels, events = out_ref.shape
    device = lax.axis_index("rows") * lax.axis_size("cols") + lax.axis_index("cols")
    second = device % 2
    blocks = [ref[at:at + channels] for ref in panel_refs for at in range(0, ref.shape[0], channels)]
    for value, place in zip(blocks, places):
        at = pl.multiple_of((place + second * (4 - 2 * place)) * events, events)
        high = value.astype(jnp.bfloat16)
        window_ref[:channels, pl.ds(at, events)] = high
        window_ref[channels:, pl.ds(at, events)] = (value - high.astype(jnp.float32)).astype(jnp.bfloat16)

    def clear(at, width):
        window_ref[:, pl.ds(pl.multiple_of(at, events), width)] = jnp.zeros((2 * channels, width), jnp.bfloat16)

    for edge in range(2):
        @pl.when(device == edge)
        def _():
            clear(0, (2 - edge) * events)

        @pl.when(device == count - 1 - edge)
        def _():
            clear((3 + edge) * events, (2 - edge) * events)

    for part in range(events // BLOCK):
        rows = slice(part * BLOCK, (part + 1) * BLOCK)
        window = window_ref[:, part * BLOCK:part * BLOCK + SPAN]
        both = lax.dot_general(window, high_ref[rows], NT, preferred_element_type=jnp.float32)
        rest = lax.dot_general(window[:channels], low_ref[rows], NT, preferred_element_type=jnp.float32)
        total = both[:channels] + (both[channels:] + rest)
        out_ref[:, rows] = 0.9 * total + 0.1 * seeds_ref[:, rows]


def apply(matrix, seeds, panels, places, count):
    channels, events = seeds.shape
    return pl.pallas_call(
        functools.partial(apply_kernel, places=places, count=count),
        out_shape=jax.ShapeDtypeStruct(seeds.shape, jnp.float32),
        scratch_shapes=[pltpu.VMEM((2 * channels, 5 * events), jnp.bfloat16)],
        compiler_params=pltpu.CompilerParams(vmem_limit_bytes=32 * 2**20),
        cost_estimate=pl.CostEstimate(flops=6 * channels * events * SPAN, bytes_accessed=4 * events * SPAN, transcendentals=0),
        name="apply",
    )(*matrix, seeds, *panels)


def pack_kernel(offsets_ref, weights_ref, out_ref):
    slots = offsets_ref.shape[0]
    out_ref[:slots] = offsets_ref[...].astype(jnp.float32)
    out_ref[slots:] = weights_ref[...]


def pack(offsets, weights):
    slots, events = offsets.shape
    return pl.pallas_call(
        pack_kernel,
        out_shape=jax.ShapeDtypeStruct((2 * slots, events), jnp.float32),
        name="pack",
    )(offsets, weights)


def on_device(offsets, weights, seeds, *, count):
    channels = seeds.shape[0]
    on_chip = [(i, i ^ 1) for i in range(count)]
    ring = lambda step: [(i, (i + step - 2 * step * (i % 2)) % count) for i in range(count)]
    edges = pack(offsets, weights)
    edges = lax.all_to_all(edges, "cols", split_axis=1, concat_axis=0, tiled=True)
    matrix = build(edges)
    scores = seeds
    for step in range(ITERS):
        near = lax.ppermute(scores, AXES, ring(-1))
        pair = lax.ppermute(scores, AXES, on_chip)
        away = lax.ppermute(scores, AXES, ring(2))
        if step == 0:
            near, away, *matrix = lax.optimization_barrier((near, away, *matrix))
        cross = lax.ppermute(near, AXES, on_chip)
        scores = apply(matrix, seeds, [scores, pair, near, away, cross], (2, 3, 1, 0, 4), count)
    return scores


def solution(mesh):
    count = mesh.shape["rows"] * mesh.shape["cols"]
    in_specs = (P("cols", "rows"), P("cols", "rows"), P(None, AXES))
    return jax.shard_map(
        functools.partial(on_device, count=count),
        mesh=mesh, in_specs=in_specs, out_specs=P(None, AXES), check_vma=False,
    )
```

```python
import functools

import jax
import jax.numpy as jnp
from jax import lax
from jax.experimental import pallas as pl
from jax.experimental.pallas import tpu as pltpu
from jax.sharding import PartitionSpec as P

HW = 1024
ITERS = 3
LANES = 128
BLOCK = 256
TILES = (BLOCK + 2 * HW) // LANES
SPAN = TILES * LANES
AXES = ("rows", "cols")
NT = (((1,), (1,)), ((), ()))


def build_kernel(edges_ref, high_ref, low_ref, tile_ref, lane_ref, whigh_ref, wlow_ref):
    events = edges_ref.shape[1]
    lane = lax.broadcasted_iota(jnp.int32, (LANES, LANES), 1)
    row = lax.broadcasted_iota(jnp.int32, (LANES, LANES), 0)
    is_offset = (lane & 4) == 0
    for part in range(events // LANES):
        rows = slice(part * LANES, (part + 1) * LANES)
        cells = edges_ref[:, rows]
        turned = jnp.concatenate([cells, cells], axis=0).T
        offset = jnp.where(is_offset, turned, pltpu.roll(turned, 4, 1)).astype(jnp.int32)
        weight = jnp.where(is_offset, pltpu.roll(turned, LANES - 4, 1), turned)
        place = offset + row + (HW + part * LANES % BLOCK)
        tile_ref[rows] = (place >> 7).astype(jnp.float32)
        lane_ref[rows] = (place & (LANES - 1)).astype(jnp.float32)
        high = weight.astype(jnp.bfloat16).astype(jnp.float32)
        whigh_ref[rows] = high
        wlow_ref[rows] = weight - high

    sub = lax.broadcasted_iota(jnp.int32, (8, LANES), 0)
    lane8 = lax.broadcasted_iota(jnp.int32, (8, LANES), 1)
    owner = (lane8 >> 6) * 2 + ((lane8 >> 2) & 1)
    masks = [sub == owner, sub == owner + 4]
    lane_ids = lax.broadcasted_iota(jnp.int32, (LANES, LANES), 0).astype(jnp.float32).astype(jnp.bfloat16)
    two = lax.broadcasted_iota(jnp.int32, (16, LANES), 0)
    two = (two >> 3).astype(jnp.float32).astype(jnp.bfloat16)
    one = jnp.ones((), jnp.bfloat16)
    zero = jnp.zeros((), jnp.bfloat16)

    def eight(at):
        tile, lanes, whigh, wlow = (ref[pl.ds(at, 8), :] for ref in (tile_ref, lane_ref, whigh_ref, wlow_ref))
        twice = lambda x: jnp.concatenate([x, x], axis=0).astype(jnp.bfloat16)
        wh, wl = twice(whigh), twice(wlow)
        left, right = [], []
        highs, lows = [], []
        for mask in masks:
            mine = twice(jnp.where(mask, tile, -1.0)) - two
            hits = [mine == jnp.asarray(2.0 * step, jnp.bfloat16) for step in range(TILES // 2)]
            highs.append(jnp.concatenate([jnp.where(hit, wh, zero) for hit in hits], axis=0))
            lows.append(jnp.concatenate([jnp.where(hit, wl, zero) for hit in hits], axis=0))
            spot = jnp.sum(jnp.where(mask, lanes, 0.0), axis=0, keepdims=True)
            spot = jnp.broadcast_to(spot, (LANES, LANES)).astype(jnp.bfloat16)
            right.append(jnp.where(spot == lane_ids, one, zero))
        left = jnp.concatenate(highs + lows, axis=1)
        right = jnp.concatenate(right + right, axis=1)
        return lax.dot_general(left, right, NT, preferred_element_type=jnp.float32)

    def sixteen(turn, _):
        at = pl.multiple_of(turn * 16, 16)
        first, second = eight(at), eight(at + 8)
        for step in range(TILES):
            both = jnp.concatenate([first[step * 8:step * 8 + 8], second[step * 8:step * 8 + 8]], axis=0)
            high = both.astype(jnp.bfloat16)
            columns = slice(step * LANES, (step + 1) * LANES)
            high_ref[pl.ds(at, 16), columns] = high
            low_ref[pl.ds(at, 16), columns] = (both - high.astype(jnp.float32)).astype(jnp.bfloat16)
        return 0

    lax.fori_loop(0, events // 16, sixteen, 0, unroll=8)


def build(edges):
    events = edges.shape[1]
    out = jax.ShapeDtypeStruct((events, SPAN), jnp.bfloat16)
    return pl.pallas_call(
        build_kernel,
        out_shape=(out, out),
        scratch_shapes=[pltpu.VMEM((events, LANES), jnp.float32)] * 4,
        compiler_params=pltpu.CompilerParams(vmem_limit_bytes=32 * 2**20),
        cost_estimate=pl.CostEstimate(flops=3000000000, bytes_accessed=4 * events * SPAN, transcendentals=0),
        name="build",
    )(edges)


def split(ref, at, value):
    channels, events = value.shape
    at = pl.multiple_of(at, events)
    high = value.astype(jnp.bfloat16)
    ref[:channels, pl.ds(at, events)] = high
    ref[channels:, pl.ds(at, events)] = (value - high.astype(jnp.float32)).astype(jnp.bfloat16)


def product(window, high, low):
    channels = window.shape[0] // 2
    both = lax.dot_general(window, high, NT, preferred_element_type=jnp.float32)
    rest = lax.dot_general(window[:channels], low, NT, preferred_element_type=jnp.float32)
    return both[:channels] + (both[channels:] + rest)


def chip_kernel(high_ref, low_ref, seeds_ref, own_ref, pair_ref, out_ref, window_ref):
    events = out_ref.shape[1]
    second = lax.axis_index("cols") % 2
    split(window_ref, second * events, own_ref[...])
    split(window_ref, (1 - second) * events, pair_ref[...])
    for part in range(events // BLOCK):
        rows = slice(part * BLOCK, (part + 1) * BLOCK)
        columns = pl.ds(pl.multiple_of((2 - second) * events - part * BLOCK, BLOCK), 2 * events)
        total = product(window_ref[...], high_ref[rows, columns], low_ref[rows, columns])
        out_ref[:, rows] = 0.9 * total + 0.1 * seeds_ref[:, rows]


def far_kernel(high_ref, low_ref, part_ref, *refs, places, count):
    *panel_refs, out_ref, window_ref = refs
    channels, events = out_ref.shape
    device = lax.axis_index("rows") * lax.axis_size("cols") + lax.axis_index("cols")
    second = device % 2
    blocks = [ref[at:at + channels] for ref in panel_refs for at in range(0, ref.shape[0], channels)]
    for value, place in zip(blocks, places):
        split(window_ref, (place + second * (4 - 2 * place)) * events, value)

    def clear(at, width):
        window_ref[:, pl.ds(pl.multiple_of(at, events), width)] = jnp.zeros((2 * channels, width), jnp.bfloat16)

    for edge in range(2):
        @pl.when(device == edge)
        def _():
            clear(0, (2 - edge) * events)

        @pl.when(device == count - 1 - edge)
        def _():
            clear((3 + edge) * events, (2 - edge) * events)

    for core in range(2):
        @pl.when(second == core)
        def _():
            here = (2 - core) * events
            for part in range(events // BLOCK):
                rows = slice(part * BLOCK, (part + 1) * BLOCK)
                total = part_ref[:, rows]
                for first, last in ((part * BLOCK, here), (here + 2 * events, part * BLOCK + SPAN)):
                    columns = slice(first - part * BLOCK, last - part * BLOCK)
                    total += 0.9 * product(window_ref[:, first:last], high_ref[rows, columns], low_ref[rows, columns])
                out_ref[:, rows] = total


def call(kernel, name, seeds, width, *args):
    channels, events = seeds.shape
    return pl.pallas_call(
        kernel,
        out_shape=jax.ShapeDtypeStruct(seeds.shape, jnp.float32),
        scratch_shapes=[pltpu.VMEM((2 * channels, width * events), jnp.bfloat16)],
        compiler_params=pltpu.CompilerParams(vmem_limit_bytes=32 * 2**20),
        cost_estimate=pl.CostEstimate(flops=3 * channels * events * SPAN, bytes_accessed=2 * events * SPAN, transcendentals=0),
        name=name,
    )(*args)


def chip_part(matrix, seeds, own, pair):
    return call(chip_kernel, "chip_part", seeds, 2, *matrix, seeds, own, pair)


def far_part(matrix, seeds, part, panels, places, count):
    kernel = functools.partial(far_kernel, places=places, count=count)
    return call(kernel, "far_part", seeds, 5, *matrix, part, *panels)


def pack_kernel(offsets_ref, weights_ref, out_ref):
    slots = offsets_ref.shape[0]
    out_ref[:slots] = offsets_ref[...].astype(jnp.float32)
    out_ref[slots:] = weights_ref[...]


def pack(offsets, weights):
    slots, events = offsets.shape
    return pl.pallas_call(
        pack_kernel,
        out_shape=jax.ShapeDtypeStruct((2 * slots, events), jnp.float32),
        name="pack",
    )(offsets, weights)


def on_device(offsets, weights, seeds, *, count):
    channels = seeds.shape[0]
    on_chip = [(i, i ^ 1) for i in range(count)]
    ring = lambda step: [(i, (i + step - 2 * step * (i % 2)) % count) for i in range(count)]
    skip = [(i, i + 2 - 4 * (i % 2)) for i in range(count) if 0 <= i + 2 - 4 * (i % 2) < count] + [(1, 0), (count - 2, count - 1)]
    edges = pack(offsets, weights)
    edges = lax.all_to_all(edges, "cols", split_axis=1, concat_axis=0, tiled=True)
    matrix = build(edges)
    scores = seeds
    for step in range(ITERS):
        pair = lax.ppermute(scores, AXES, on_chip)
        near = lax.ppermute(scores, AXES, ring(-1))
        away = lax.ppermute(scores, AXES, skip if step == 0 else ring(3))
        part = chip_part(matrix, seeds, scores, pair)
        if step == 0:
            near, away, part = lax.optimization_barrier((near, away, part))
            cross = lax.ppermute(near, AXES, on_chip)
            scores = far_part(matrix, seeds, part, [away, near, cross], (0, 1, 4), count)
        else:
            near, away, part = lax.optimization_barrier((near, away, part))
            cross = lax.ppermute(jnp.concatenate([near, away], axis=0), AXES, on_chip)
            scores = far_part(matrix, seeds, part, [near, cross], (1, 4, 0), count)
    return scores


def solution(mesh):
    count = mesh.shape["rows"] * mesh.shape["cols"]
    in_specs = (P("cols", "rows"), P("cols", "rows"), P(None, AXES))
    return jax.shard_map(
        functools.partial(on_device, count=count),
        mesh=mesh, in_specs=in_specs, out_specs=P(None, AXES), check_vma=False,
    )
```

```python
import functools

import jax
import jax.numpy as jnp
from jax import lax
from jax.experimental import pallas as pl
from jax.experimental.pallas import tpu as pltpu
from jax.sharding import PartitionSpec as P

HW = 1024
ITERS = 3
LANES = 128
BLOCK = 256
TILES = (BLOCK + 2 * HW) // LANES
SPAN = TILES * LANES
AXES = ("rows", "cols")
NT = (((1,), (1,)), ((), ()))


def build_kernel(edges_ref, high_ref, low_ref, tile_ref, lane_ref, whigh_ref, wlow_ref):
    events = edges_ref.shape[1]
    lane = lax.broadcasted_iota(jnp.int32, (LANES, LANES), 1)
    row = lax.broadcasted_iota(jnp.int32, (LANES, LANES), 0)
    is_offset = (lane & 4) == 0
    for part in range(events // LANES):
        rows = slice(part * LANES, (part + 1) * LANES)
        cells = edges_ref[:, rows]
        turned = jnp.concatenate([cells, cells], axis=0).T
        offset = jnp.where(is_offset, turned, pltpu.roll(turned, 4, 1)).astype(jnp.int32)
        weight = jnp.where(is_offset, pltpu.roll(turned, LANES - 4, 1), turned)
        place = offset + row + (HW + part * LANES % BLOCK)
        tile_ref[rows] = (place >> 7).astype(jnp.float32)
        lane_ref[rows] = (place & (LANES - 1)).astype(jnp.float32)
        high = weight.astype(jnp.bfloat16).astype(jnp.float32)
        whigh_ref[rows] = high
        wlow_ref[rows] = weight - high

    sub = lax.broadcasted_iota(jnp.int32, (8, LANES), 0)
    lane8 = lax.broadcasted_iota(jnp.int32, (8, LANES), 1)
    owner = (lane8 >> 6) * 2 + ((lane8 >> 2) & 1)
    masks = [sub == owner, sub == owner + 4]
    lane_ids = lax.broadcasted_iota(jnp.int32, (LANES, LANES), 0).astype(jnp.float32).astype(jnp.bfloat16)
    two = lax.broadcasted_iota(jnp.int32, (16, LANES), 0)
    two = (two >> 3).astype(jnp.float32).astype(jnp.bfloat16)
    one = jnp.ones((), jnp.bfloat16)
    zero = jnp.zeros((), jnp.bfloat16)

    def eight(at):
        tile, lanes, whigh, wlow = (ref[pl.ds(at, 8), :] for ref in (tile_ref, lane_ref, whigh_ref, wlow_ref))
        twice = lambda x: jnp.concatenate([x, x], axis=0).astype(jnp.bfloat16)
        wh, wl = twice(whigh), twice(wlow)
        left, right = [], []
        highs, lows = [], []
        for mask in masks:
            mine = twice(jnp.where(mask, tile, -1.0)) - two
            hits = [mine == jnp.asarray(2.0 * step, jnp.bfloat16) for step in range(TILES // 2)]
            highs.append(jnp.concatenate([jnp.where(hit, wh, zero) for hit in hits], axis=0))
            lows.append(jnp.concatenate([jnp.where(hit, wl, zero) for hit in hits], axis=0))
            spot = jnp.sum(jnp.where(mask, lanes, 0.0), axis=0, keepdims=True)
            spot = jnp.broadcast_to(spot, (LANES, LANES)).astype(jnp.bfloat16)
            right.append(jnp.where(spot == lane_ids, one, zero))
        left = jnp.concatenate(highs + lows, axis=1)
        right = jnp.concatenate(right + right, axis=1)
        return lax.dot_general(left, right, NT, preferred_element_type=jnp.float32)

    def sixteen(turn, _):
        at = pl.multiple_of(turn * 16, 16)
        first, second = eight(at), eight(at + 8)
        for step in range(TILES):
            both = jnp.concatenate([first[step * 8:step * 8 + 8], second[step * 8:step * 8 + 8]], axis=0)
            high = both.astype(jnp.bfloat16)
            columns = slice(step * LANES, (step + 1) * LANES)
            high_ref[pl.ds(at, 16), columns] = high
            low_ref[pl.ds(at, 16), columns] = (both - high.astype(jnp.float32)).astype(jnp.bfloat16)
        return 0

    lax.fori_loop(0, events // 16, sixteen, 0, unroll=16)


def build(edges):
    events = edges.shape[1]
    out = jax.ShapeDtypeStruct((events, SPAN), jnp.bfloat16)
    return pl.pallas_call(
        build_kernel,
        out_shape=(out, out),
        scratch_shapes=[pltpu.VMEM((events, LANES), jnp.float32)] * 4,
        compiler_params=pltpu.CompilerParams(vmem_limit_bytes=32 * 2**20),
        cost_estimate=pl.CostEstimate(flops=3000000000, bytes_accessed=4 * events * SPAN, transcendentals=0),
        name="build",
    )(edges)


def split(ref, at, value):
    channels, events = value.shape
    at = pl.multiple_of(at, events)
    high = value.astype(jnp.bfloat16)
    ref[:channels, pl.ds(at, events)] = high
    ref[channels:, pl.ds(at, events)] = (value - high.astype(jnp.float32)).astype(jnp.bfloat16)


def product(window, high, low):
    channels = window.shape[0] // 2
    both = lax.dot_general(window, high, NT, preferred_element_type=jnp.float32)
    rest = lax.dot_general(window[:channels], low, NT, preferred_element_type=jnp.float32)
    return both[:channels] + (both[channels:] + rest)


def chip_kernel(high_ref, low_ref, seeds_ref, own_ref, pair_ref, out_ref, window_ref):
    events = out_ref.shape[1]
    second = lax.axis_index("cols") % 2
    split(window_ref, second * events, own_ref[...])
    split(window_ref, (1 - second) * events, pair_ref[...])
    for part in range(events // BLOCK):
        rows = slice(part * BLOCK, (part + 1) * BLOCK)
        columns = pl.ds(pl.multiple_of((2 - second) * events - part * BLOCK, BLOCK), 2 * events)
        total = product(window_ref[...], high_ref[rows, columns], low_ref[rows, columns])
        out_ref[:, rows] = 0.9 * total + 0.1 * seeds_ref[:, rows]


def far_kernel(high_ref, low_ref, part_ref, *refs, places, count):
    *panel_refs, out_ref, window_ref = refs
    channels, events = out_ref.shape
    device = lax.axis_index("rows") * lax.axis_size("cols") + lax.axis_index("cols")
    second = device % 2
    blocks = [ref[at:at + channels] for ref in panel_refs for at in range(0, ref.shape[0], channels)]
    for value, place in zip(blocks, places):
        split(window_ref, (place + second * (4 - 2 * place)) * events, value)

    def clear(at, width):
        window_ref[:, pl.ds(pl.multiple_of(at, events), width)] = jnp.zeros((2 * channels, width), jnp.bfloat16)

    for edge in range(2):
        @pl.when(device == edge)
        def _():
            clear(0, (2 - edge) * events)

        @pl.when(device == count - 1 - edge)
        def _():
            clear((3 + edge) * events, (2 - edge) * events)

    for core in range(2):
        @pl.when(second == core)
        def _():
            here = (2 - core) * events
            for part in range(events // BLOCK):
                rows = slice(part * BLOCK, (part + 1) * BLOCK)
                total = part_ref[:, rows]
                for first, last in ((part * BLOCK, here), (here + 2 * events, part * BLOCK + SPAN)):
                    columns = slice(first - part * BLOCK, last - part * BLOCK)
                    total += 0.9 * product(window_ref[:, first:last], high_ref[rows, columns], low_ref[rows, columns])
                out_ref[:, rows] = total


def call(kernel, name, seeds, width, *args):
    channels, events = seeds.shape
    return pl.pallas_call(
        kernel,
        out_shape=jax.ShapeDtypeStruct(seeds.shape, jnp.float32),
        scratch_shapes=[pltpu.VMEM((2 * channels, width * events), jnp.bfloat16)],
        compiler_params=pltpu.CompilerParams(vmem_limit_bytes=32 * 2**20),
        cost_estimate=pl.CostEstimate(flops=3 * channels * events * SPAN, bytes_accessed=2 * events * SPAN, transcendentals=0),
        name=name,
    )(*args)


def chip_part(matrix, seeds, own, pair):
    return call(chip_kernel, "chip_part", seeds, 2, *matrix, seeds, own, pair)


def far_part(matrix, seeds, part, panels, places, count):
    kernel = functools.partial(far_kernel, places=places, count=count)
    return call(kernel, "far_part", seeds, 5, *matrix, part, *panels)


def pack_kernel(offsets_ref, weights_ref, out_ref):
    slots = offsets_ref.shape[0]
    out_ref[:slots] = offsets_ref[...].astype(jnp.float32)
    out_ref[slots:] = weights_ref[...]


def pack(offsets, weights):
    slots, events = offsets.shape
    return pl.pallas_call(
        pack_kernel,
        out_shape=jax.ShapeDtypeStruct((2 * slots, events), jnp.float32),
        name="pack",
    )(offsets, weights)


def on_device(offsets, weights, seeds, *, count):
    channels = seeds.shape[0]
    on_chip = [(i, i ^ 1) for i in range(count)]
    ring = lambda step: [(i, (i + step - 2 * step * (i % 2)) % count) for i in range(count)]
    skip = [(i, i + 2 - 4 * (i % 2)) for i in range(count) if 0 <= i + 2 - 4 * (i % 2) < count] + [(1, 0), (count - 2, count - 1)]
    edges = pack(offsets, weights)
    edges = lax.all_to_all(edges, "cols", split_axis=1, concat_axis=0, tiled=True)
    matrix = build(edges)
    scores = seeds
    for step in range(ITERS):
        pair = lax.ppermute(scores, AXES, on_chip)
        near = lax.ppermute(scores, AXES, ring(-1))
        away = lax.ppermute(scores, AXES, skip if step == 0 else ring(3))
        part = chip_part(matrix, seeds, scores, pair)
        if step == 0:
            near, away, part = lax.optimization_barrier((near, away, part))
            cross = lax.ppermute(near, AXES, on_chip)
            scores = far_part(matrix, seeds, part, [away, near, cross], (0, 1, 4), count)
        else:
            near, away, part = lax.optimization_barrier((near, away, part))
            cross = lax.ppermute(jnp.concatenate([near, away], axis=0), AXES, on_chip)
            scores = far_part(matrix, seeds, part, [near, cross], (1, 4, 0), count)
    return scores


def solution(mesh):
    count = mesh.shape["rows"] * mesh.shape["cols"]
    in_specs = (P("cols", "rows"), P("cols", "rows"), P(None, AXES))
    return jax.shard_map(
        functools.partial(on_device, count=count),
        mesh=mesh, in_specs=in_specs, out_specs=P(None, AXES), check_vma=False,
    )
```

```python
import functools

import jax
import jax.numpy as jnp
from jax import lax
from jax.experimental import pallas as pl
from jax.experimental.pallas import tpu as pltpu
from jax.sharding import PartitionSpec as P

HW = 1024
ITERS = 3
LANES = 128
BLOCK = 256
TILES = (BLOCK + 2 * HW) // LANES
SPAN = TILES * LANES
AXES = ("rows", "cols")
NT = (((1,), (1,)), ((), ()))


def build_kernel(edges_ref, high_ref, low_ref, tile_ref, lane_ref, whigh_ref, wlow_ref):
    events = edges_ref.shape[1]
    lane = lax.broadcasted_iota(jnp.int32, (LANES, LANES), 1)
    row = lax.broadcasted_iota(jnp.int32, (LANES, LANES), 0)
    is_offset = (lane & 4) == 0
    for part in range(events // LANES):
        rows = slice(part * LANES, (part + 1) * LANES)
        cells = edges_ref[:, rows]
        turned = jnp.concatenate([cells, cells], axis=0).T
        offset = jnp.where(is_offset, turned, pltpu.roll(turned, 4, 1)).astype(jnp.int32)
        weight = jnp.where(is_offset, pltpu.roll(turned, LANES - 4, 1), turned)
        place = offset + row + (HW + part * LANES % BLOCK)
        tile_ref[rows] = (place >> 7).astype(jnp.float32)
        lane_ref[rows] = (place & (LANES - 1)).astype(jnp.float32)
        high = weight.astype(jnp.bfloat16).astype(jnp.float32)
        whigh_ref[rows] = high
        wlow_ref[rows] = weight - high

    sub = lax.broadcasted_iota(jnp.int32, (8, LANES), 0)
    lane8 = lax.broadcasted_iota(jnp.int32, (8, LANES), 1)
    owner = (lane8 >> 6) * 2 + ((lane8 >> 2) & 1)
    masks = [sub == owner, sub == owner + 4]
    lane_ids = lax.broadcasted_iota(jnp.int32, (LANES, LANES), 0).astype(jnp.float32).astype(jnp.bfloat16)
    two = lax.broadcasted_iota(jnp.int32, (16, LANES), 0)
    two = (two >> 3).astype(jnp.float32).astype(jnp.bfloat16)
    one = jnp.ones((), jnp.bfloat16)
    zero = jnp.zeros((), jnp.bfloat16)

    def eight(at):
        tile, lanes, whigh, wlow = (ref[pl.ds(at, 8), :] for ref in (tile_ref, lane_ref, whigh_ref, wlow_ref))
        twice = lambda x: jnp.concatenate([x, x], axis=0).astype(jnp.bfloat16)
        wh, wl = twice(whigh), twice(wlow)
        left, right = [], []
        highs, lows = [], []
        for mask in masks:
            mine = twice(jnp.where(mask, tile, -1.0)) - two
            hits = [mine == jnp.asarray(2.0 * step, jnp.bfloat16) for step in range(TILES // 2)]
            highs.append(jnp.concatenate([jnp.where(hit, wh, zero) for hit in hits], axis=0))
            lows.append(jnp.concatenate([jnp.where(hit, wl, zero) for hit in hits], axis=0))
            spot = jnp.sum(jnp.where(mask, lanes, 0.0), axis=0, keepdims=True)
            spot = jnp.broadcast_to(spot, (LANES, LANES)).astype(jnp.bfloat16)
            right.append(jnp.where(spot == lane_ids, one, zero))
        left = jnp.concatenate(highs + lows, axis=1)
        right = jnp.concatenate(right + right, axis=1)
        return lax.dot_general(left, right, NT, preferred_element_type=jnp.float32)

    def sixteen(turn, _):
        at = pl.multiple_of(turn * 16, 16)
        first, second = eight(at), eight(at + 8)
        for step in range(TILES):
            both = jnp.concatenate([first[step * 8:step * 8 + 8], second[step * 8:step * 8 + 8]], axis=0)
            high = both.astype(jnp.bfloat16)
            columns = slice(step * LANES, (step + 1) * LANES)
            high_ref[pl.ds(at, 16), columns] = high
            low_ref[pl.ds(at, 16), columns] = (both - high.astype(jnp.float32)).astype(jnp.bfloat16)
        return 0

    lax.fori_loop(0, events // 16, sixteen, 0, unroll=16)


def build(edges):
    events = edges.shape[1]
    out = jax.ShapeDtypeStruct((events, SPAN), jnp.bfloat16)
    return pl.pallas_call(
        build_kernel,
        out_shape=(out, out),
        scratch_shapes=[pltpu.VMEM((events, LANES), jnp.float32)] * 4,
        compiler_params=pltpu.CompilerParams(vmem_limit_bytes=32 * 2**20),
        cost_estimate=pl.CostEstimate(flops=3000000000, bytes_accessed=4 * events * SPAN, transcendentals=0),
        name="build",
    )(edges)


def split(ref, at, value):
    channels, events = value.shape
    at = pl.multiple_of(at, events)
    high = value.astype(jnp.bfloat16)
    ref[:channels, pl.ds(at, events)] = high
    ref[channels:, pl.ds(at, events)] = (value - high.astype(jnp.float32)).astype(jnp.bfloat16)


def product(window, high, low):
    channels = window.shape[0] // 2
    both = lax.dot_general(window, high, NT, preferred_element_type=jnp.float32)
    rest = lax.dot_general(window[:channels], low, NT, preferred_element_type=jnp.float32)
    return both[:channels] + (both[channels:] + rest)


def chip_kernel(high_ref, low_ref, seeds_ref, own_ref, pair_ref, out_ref, window_ref):
    events = out_ref.shape[1]
    second = lax.axis_index("cols") % 2
    split(window_ref, second * events, own_ref[...])
    split(window_ref, (1 - second) * events, pair_ref[...])
    for part in range(events // BLOCK):
        rows = slice(part * BLOCK, (part + 1) * BLOCK)
        columns = pl.ds(pl.multiple_of((2 - second) * events - part * BLOCK, BLOCK), 2 * events)
        total = product(window_ref[...], high_ref[rows, columns], low_ref[rows, columns])
        out_ref[:, rows] = 0.9 * total + 0.1 * seeds_ref[:, rows]


def far_kernel(high_ref, low_ref, part_ref, *refs, places, count):
    *panel_refs, out_ref, window_ref = refs
    channels, events = out_ref.shape
    device = lax.axis_index("rows") * lax.axis_size("cols") + lax.axis_index("cols")
    second = device % 2
    blocks = [ref[at:at + channels] for ref in panel_refs for at in range(0, ref.shape[0], channels)]
    for value, place in zip(blocks, places):
        split(window_ref, (place + second * (4 - 2 * place)) * events, value)

    def clear(at, width):
        window_ref[:, pl.ds(pl.multiple_of(at, events), width)] = jnp.zeros((2 * channels, width), jnp.bfloat16)

    for edge in range(2):
        @pl.when(device == edge)
        def _():
            clear(0, (2 - edge) * events)

        @pl.when(device == count - 1 - edge)
        def _():
            clear((3 + edge) * events, (2 - edge) * events)

    for core in range(2):
        @pl.when(second == core)
        def _():
            here = (2 - core) * events
            for part in range(events // BLOCK):
                rows = slice(part * BLOCK, (part + 1) * BLOCK)
                total = part_ref[:, rows]
                for first, last in ((part * BLOCK, here), (here + 2 * events, part * BLOCK + SPAN)):
                    columns = slice(first - part * BLOCK, last - part * BLOCK)
                    total += 0.9 * product(window_ref[:, first:last], high_ref[rows, columns], low_ref[rows, columns])
                out_ref[:, rows] = total


def call(kernel, name, seeds, width, *args):
    channels, events = seeds.shape
    return pl.pallas_call(
        kernel,
        out_shape=jax.ShapeDtypeStruct(seeds.shape, jnp.float32),
        scratch_shapes=[pltpu.VMEM((2 * channels, width * events), jnp.bfloat16)],
        compiler_params=pltpu.CompilerParams(vmem_limit_bytes=32 * 2**20),
        cost_estimate=pl.CostEstimate(flops=3 * channels * events * SPAN, bytes_accessed=2 * events * SPAN, transcendentals=0),
        name=name,
    )(*args)


def chip_part(matrix, seeds, own, pair):
    return call(chip_kernel, "chip_part", seeds, 2, *matrix, seeds, own, pair)


def far_part(matrix, seeds, part, panels, places, count):
    kernel = functools.partial(far_kernel, places=places, count=count)
    return call(kernel, "far_part", seeds, 5, *matrix, part, *panels)


def pack_kernel(offsets_ref, weights_ref, out_ref):
    slots = offsets_ref.shape[0]
    out_ref[:slots] = offsets_ref[...].astype(jnp.float32)
    out_ref[slots:] = weights_ref[...]


def pack(offsets, weights):
    slots, events = offsets.shape
    return pl.pallas_call(
        pack_kernel,
        out_shape=jax.ShapeDtypeStruct((2 * slots, events), jnp.float32),
        name="pack",
    )(offsets, weights)


def on_device(offsets, weights, seeds, *, count):
    channels = seeds.shape[0]
    on_chip = [(i, i ^ 1) for i in range(count)]
    ring = lambda step: [(i, (i + step - 2 * step * (i % 2)) % count) for i in range(count)]
    skip = [(i, i + 2 - 4 * (i % 2)) for i in range(count) if 0 <= i + 2 - 4 * (i % 2) < count] + [(1, 0), (count - 2, count - 1)]
    edges = pack(offsets, weights)
    edges = lax.all_to_all(edges, "cols", split_axis=1, concat_axis=0, tiled=True)
    matrix = build(edges)
    scores = seeds
    for step in range(ITERS):
        pair = lax.ppermute(scores, AXES, on_chip)
        near = lax.ppermute(scores, AXES, ring(-1))
        away = lax.ppermute(scores, AXES, skip if step == 0 else ring(3))
        part = chip_part(matrix, seeds, scores, pair)
        if step == 0:
            near, away, part = lax.optimization_barrier((near, away, part))
            cross = lax.ppermute(near, AXES, on_chip)
            scores = far_part(matrix, seeds, part, [away, near, cross], (0, 1, 4), count)
        else:
            near, away, part = lax.optimization_barrier((near, away, part))
            cross = [lax.ppermute(block, AXES, on_chip) for block in (near, away)]
            scores = far_part(matrix, seeds, part, [near, *cross], (1, 4, 0), count)
    return scores


def solution(mesh):
    count = mesh.shape["rows"] * mesh.shape["cols"]
    in_specs = (P("cols", "rows"), P("cols", "rows"), P(None, AXES))
    return jax.shard_map(
        functools.partial(on_device, count=count),
        mesh=mesh, in_specs=in_specs, out_specs=P(None, AXES), check_vma=False,
    )
```
